32 devices in a mesh: pole: 2 (over y), col: 4 (over z), row: 4 (over x, core).
Axes of the slice: x: 2, y: 2, z: 4, core: 2. Of those that a mesh axis runs over, the one named last changes fastest.
Arguments:
- ancestor_inverse: bfloat16 [4, 2048, 2048], P('pole', 'col', 'row'), parts along dimension 0, may hold values from -0.125 to 0.125
- panels: bfloat16 [6, 2048, 512], P('pole', 'col'), parts along dimension 0, may hold values from -0.8984375 to 0.8984375
- block_lists: int32 [6, 16], P('pole'), parts along dimension 0, may hold values from -1 to 15, as said below
- diag_inverse: float32 [6, 256, 512], P('pole', ('col', 'row')), parts along dimension 0, may hold values from -6 to 6
Outputs:
- offdiag: bfloat16 [6, 2048, 512], P('pole', ('col', 'row')), parts along dimension 0
- diag_block: float32 [6, 256, 512], P('pole', ('col', 'row')), parts along dimension 0
The draws below stay inside these ranges and needn't reach their ends.
There are 2 independent parts, one for each index of `pole`. The reference program is written for one: setup_inputs(seed, part) draws one part's arguments, and reference() takes and returns one part's arrays. A program takes and returns all parts, laid end to end along the dimension named above; each array names one. Nothing has to cross between parts.
Inputs may be any that keep to these rules, and one draw needn't show every extreme that they name: `block_lists`: in every supernode, the slots of range r hold distinct blocks of r * 4 to r * 4 + 3, filled slots first and -1 after them; every range has at least one filled slot, and some range has all 4 filled.
All inputs are finite; a program needn't handle non-finite values.
Results may differ from the reference program's by a relative error of at most 0.017.
Values may be sent and summed in bfloat16 or wider, within the bound.
A program may use at most 64 MiB of HBM per device.

```python
import jax
import jax.numpy as jnp
from jax import lax

W = 256
BS = 128
BPR = 4
CAP = 4
NSUP = 3
GRID = 4
M = 2048
SLOTS = 16


def draw_block_lists(key, part):
    key_count = jax.random.fold_in(key, 11)
    key_full = jax.random.fold_in(key, 12)
    key_order = jax.random.fold_in(key, 13)
    counts = jax.random.randint(key_count, (NSUP, GRID), 1, CAP + 1)
    full_range = jax.random.randint(key_full, (NSUP,), 0, GRID)
    ranges = jnp.arange(GRID, dtype=jnp.int32)
    counts = jnp.where(ranges[None, :] == full_range[:, None], CAP, counts)
    scores = jax.random.randint(key_order, (NSUP, GRID, BPR), 0, 1 << 20) * BPR + jnp.arange(BPR, dtype=jnp.int32)[None, None, :]
    order = jnp.argsort(scores, axis=2)[:, :, :CAP].astype(jnp.int32)
    blocks = ranges[None, :, None] * BPR + order
    slot_ids = jnp.arange(CAP, dtype=jnp.int32)
    filled = jnp.where(slot_ids[None, None, :] < counts[:, :, None], blocks, -1)
    return filled.reshape(NSUP, GRID * CAP).astype(jnp.int32)


def block_scale(stream_key, shape, split, low, largest):
    gain = 1.0
    for axis_at, parts in split:
        steps = jax.random.uniform(jax.random.fold_in(jax.random.fold_in(stream_key, 6), axis_at), (parts,), jnp.float32, low / len(split), largest / len(split))
        gain = gain * jnp.repeat(jnp.exp(steps), shape[axis_at] // parts).reshape((-1,) + (1,) * (len(shape) - 1 - axis_at))
    return gain


def normal_values(stream_key, extent, deviation, reach, split=(), kind=jnp.bfloat16):
    entries = jax.random.normal(stream_key, extent, jnp.float32) * deviation
    if len(split) > 0:
        entries = block_scale(stream_key, extent, split, -0.22, 0.18) * entries
    return jnp.clip(entries, min=-reach, max=reach).astype(kind)


def setup_inputs(seed: int = 0, part: int = 0) -> dict:
    keys = jax.random.split(jax.random.key(seed), 5)
    part_splits = jax.random.split(jax.random.fold_in(keys[4], part), 5)
    return {
        "ancestor_inverse": normal_values(part_splits[0], (2, M, M), (SLOTS * BS) ** -0.5, 0.125, ((1, 4), (2, 4))),
        "panels": normal_values(part_splits[1], (NSUP, SLOTS * BS, 2 * W), 0.15, 0.8984375, ((1, 4),)),
        "block_lists": draw_block_lists(jax.random.fold_in(jax.random.fold_in(keys[4], part), 71), part),
        "diag_inverse": normal_values(part_splits[3], (NSUP, W, 2 * W), 1.0, 6.0, ((1, 16),), jnp.float32),
    }


def complex_product(left_real, left_imag, right):
    first = jnp.dot(left_real, right, preferred_element_type=jnp.float32)
    second = jnp.dot(left_imag, right, preferred_element_type=jnp.float32)
    return jnp.concatenate([first[:, :W] - second[:, W:], first[:, W:] + second[:, :W]], axis=1)


def reference(ancestor_inverse, panels, block_lists, diag_inverse):
    width = CAP * BS
    offdiag_all = []
    diag_all = []
    for k in range(NSUP):
        listed = block_lists[k]
        valid = (listed >= 0).astype(jnp.float32)
        row_index = (jnp.maximum(listed, 0)[:, None] * BS + jnp.arange(BS, dtype=jnp.int32)[None, :]).reshape(-1).astype(jnp.int32)
        row_mask = jnp.repeat(valid, BS)
        lhat = (panels[k].astype(jnp.float32) * row_mask[:, None]).astype(jnp.bfloat16)
        picked = jnp.take(jnp.take(ancestor_inverse, row_index, axis=1), row_index, axis=2)

        def add_range(total, range_id):
            columns = lax.dynamic_slice_in_dim(picked, range_id * width, width, 2)
            rows = lax.dynamic_slice_in_dim(lhat, range_id * width, width, 0)
            term = complex_product(columns[0], columns[1], rows) * row_mask[:, None]
            rounded = lax.optimization_barrier(term.astype(jnp.bfloat16))
            return total + rounded.astype(jnp.float32), None

        start = jnp.zeros((SLOTS * BS, 2 * W), jnp.float32)
        total, unused = lax.scan(add_range, start, jnp.arange(GRID, dtype=jnp.int32))
        offdiag = (-total).astype(jnp.bfloat16)
        update = complex_product(lhat[:, :W].T, lhat[:, W:].T, offdiag)
        offdiag_all.append(offdiag)
        diag_all.append(diag_inverse[k] - update)
    return jnp.stack(offdiag_all), jnp.stack(diag_all)
```

```python
import functools

import jax
import jax.numpy as jnp
from jax import lax
from jax.experimental import pallas as pl
from jax.experimental.pallas import tpu as pltpu
from jax.sharding import PartitionSpec as P

BS = 128
BPR = 4
CAP = 4
CORES = 2
RELAYED = 2
MESH = pl.DeviceIdType.MESH


def kernel(
    ncol,
    lists,
    inverse,
    panels,
    diag_inverse,
    offdiag,
    diag_block,
    listed,
    relay,
    turned,
    term,
    parts,
    first_in,
    second_out,
    second_in,
    third_out,
    third_own,
    third_in,
    chain_send,
    chain_recv,
    relay_send,
    relay_recv,
    cross_send,
    first_send,
    first_recv,
    second_send,
    second_recv,
    third_send,
    third_recv,
    local_sem,
):
    nsup = panels.shape[0]
    width = panels.shape[3] // 2
    deep = diag_inverse.shape[1]
    col = lax.axis_index("col")
    row = lax.axis_index("row")
    core = lax.rem(row, CORES)
    across = row // CORES
    sibling = across * CORES + (1 - core)
    opposite = (1 - across) * CORES + core
    main = range(CAP - RELAYED)
    relayed = range(CAP - RELAYED, CAP)
    ways = (1, -1)

    barrier = pltpu.get_barrier_semaphore()
    for other in (sibling, opposite):
        pl.semaphore_signal(barrier, inc=1, device_id={"row": other}, device_id_type=MESH)
    for step in range(1, ncol):
        pl.semaphore_signal(
            barrier, inc=1, device_id={"col": lax.rem(col + step, ncol)}, device_id_type=MESH
        )
    pl.semaphore_wait(barrier, ncol + 1)

    def along(source, target, send, recv, way):
        return pltpu.make_async_remote_copy(
            src_ref=source,
            dst_ref=target,
            send_sem=send,
            recv_sem=recv,
            device_id={"col": jnp.clip(col + way, 0, ncol - 1)},
            device_id_type=MESH,
        )

    def in_row(source, target, send, recv, other):
        return pltpu.make_async_remote_copy(
            src_ref=source,
            dst_ref=target,
            send_sem=send,
            recv_sem=recv,
            device_id={"row": other},
            device_id_type=MESH,
        )

    def room(way):
        return col < ncol - 1 if way > 0 else col > 0

    def beyond(origin, way):
        return col > origin if way > 0 else col < origin

    def chain_copy(source, k, s, w):
        return along(
            source, listed[k].at[s], chain_send.at[k, s, w], chain_recv.at[k, s], ways[w]
        )

    def relay_copy(source, at, k, s, w):
        i = s - relayed[0]
        return along(
            source.at[k, at], relay.at[k, i], relay_send.at[k, i, w], relay_recv.at[k, i], ways[w]
        )

    def cross_copy(k, s):
        i = s - relayed[0]
        return in_row(relay.at[k, i], listed[k].at[s], cross_send.at[k, i], chain_recv.at[k, s], opposite)

    def own_copy(k):
        return pltpu.make_async_copy(panels.at[k], listed[k], local_sem.at[k])

    for w, way in enumerate(ways):

        @pl.when((col == row) & room(way))
        def _():
            for k in range(nsup):
                for s in main:
                    chain_copy(panels.at[k, s], k, s, w).start()

        @pl.when((col == opposite) & room(way))
        def _():
            for k in range(nsup):
                for s in relayed:
                    relay_copy(panels, s, k, s, w).start()

    @pl.when(col == row)
    def _():
        for k in range(nsup):
            own_copy(k).start()

    for k in range(nsup):
        rows = jnp.concatenate(
            [panels[k, x * CORES + c] for c in range(CORES) for x in range(CAP // CORES)], axis=0
        )
        turned[k] = rows.T

    @pl.when(col == row)
    def _():
        for k in range(nsup):
            own_copy(k).wait()

    def forward(k):
        for j in range(CAP):
            if j < len(main):
                s = main[j]

                @pl.when(col != row)
                def _():
                    chain_copy(listed[k].at[s], k, s, 0).wait_recv()

                for w, way in enumerate(ways):

                    @pl.when(beyond(row, way) & room(way))
                    def _():
                        chain_copy(listed[k].at[s], k, s, w).start()

            if j < len(relayed):
                s = relayed[j]

                @pl.when(col != opposite)
                def _():
                    relay_copy(relay, s - relayed[0], k, s, 0).wait_recv()
                    cross_copy(k, s).start()

                for w, way in enumerate(ways):

                    @pl.when(beyond(opposite, way) & room(way))
                    def _():
                        relay_copy(relay, s - relayed[0], k, s, w).start()

        for s in relayed:

            @pl.when(col != row)
            def _():
                cross_copy(k, s).wait_recv()

    def first_copy(k):
        return in_row(
            parts.at[k, 1 - core], first_in.at[k], first_send.at[k], first_recv.at[k], sibling
        )

    def second_copy(k):
        return in_row(
            second_out.at[k], second_in.at[k], second_send.at[k], second_recv.at[k], opposite
        )

    def third_copy(k, step):
        target = lax.rem(col + step, ncol)
        return pltpu.make_async_remote_copy(
            src_ref=third_out.at[k, target],
            dst_ref=third_in.at[k, step - 1],
            send_sem=third_send.at[k, step - 1],
            recv_sem=third_recv.at[k, step - 1],
            device_id={"col": target},
            device_id_type=MESH,
        )

    def compute(k):
        natural = []
        for b in range(BPR):
            at = jnp.int32(0)
            found = jnp.int32(0)
            for s in range(CAP):
                hit = lists[k, row * CAP + s] == row * BPR + b
                at = jnp.where(hit, s, at)
                found = jnp.where(hit, 1, found)
            block = listed[k][at]
            natural.append(block * found.astype(jnp.float32).astype(block.dtype))
        natural = jnp.concatenate(natural, axis=0)
        both_planes = inverse[...].reshape(2 * BPR * BS, BPR * BS)
        product = jnp.dot(both_planes, natural, preferred_element_type=jnp.float32)
        first, second = product[: BPR * BS], product[BPR * BS :]
        term[:, :, :width] = (
            (first[:, :width] - second[:, width:]).astype(term.dtype).reshape(BPR, BS, width)
        )
        term[:, :, width:] = (
            (first[:, width:] + second[:, :width]).astype(term.dtype).reshape(BPR, BS, width)
        )
        slots = []
        for c in range(CORES):
            for x in range(CAP // CORES):
                block_id = lists[k, col * CAP + x * CORES + c]
                filled = (block_id >= 0).astype(jnp.float32).astype(term.dtype)
                piece = term[jnp.clip(block_id - col * BPR, 0, BPR - 1)] * filled
                parts[k, c, x, :BS] = piece
                slots.append(piece)
        slots = jnp.concatenate(slots, axis=0)
        update = jnp.dot(turned[k], slots, preferred_element_type=jnp.float32)
        first, second = update[:width], update[width:]
        update = jnp.concatenate(
            [first[:, :width] - second[:, width:], first[:, width:] + second[:, :width]], axis=1
        ).astype(parts.dtype)
        for z in range(ncol):
            for r in range(CAP):
                at = (z * CAP + r) * deep
                parts[k, r % CORES, r // CORES, BS + z * deep : BS + (z + 1) * deep] = update[at : at + deep]
        first_copy(k).start()

    def first_sum(k, x):
        return parts[k, core, x].astype(jnp.float32) + first_in[k, x].astype(jnp.float32)

    def second_stage(k):
        first_copy(k).wait_recv()
        second_out[k] = first_sum(k, 1 - across).astype(second_out.dtype)
        second_copy(k).start()

    def third_stage(k):
        second_copy(k).wait_recv()
        total = first_sum(k, across) + second_in[k].astype(jnp.float32)
        offdiag[k] = (-total[:BS]).astype(offdiag.dtype)
        third_own[k] = total[BS:].reshape(ncol, deep, 2 * width)
        third_out[k] = total[BS:].reshape(ncol, deep, 2 * width).astype(third_out.dtype)
        for step in range(1, ncol):
            third_copy(k, step).start()

    def last_stage(k):
        total = diag_inverse[k] + third_own[k, col]
        for step in range(1, ncol):
            third_copy(k, step).wait_recv()
            total += third_in[k, step - 1].astype(jnp.float32)
        diag_block[k] = total

    for k in range(nsup):
        forward(k)
        if k > 0:
            second_stage(k - 1)
        compute(k)
        if k > 0:
            third_stage(k - 1)
    second_stage(nsup - 1)
    third_stage(nsup - 1)
    for k in range(nsup):
        last_stage(k)

    for k in range(nsup):
        first_copy(k).wait_send()
        second_copy(k).wait_send()
        for step in range(1, ncol):
            third_copy(k, step).wait_send()
    for w, way in enumerate(ways):

        @pl.when((beyond(row, way) | (col == row)) & room(way))
        def _():
            for k in range(nsup):
                for s in main:
                    chain_copy(listed[k].at[s], k, s, w).wait_send()

        @pl.when((beyond(opposite, way) | (col == opposite)) & room(way))
        def _():
            for k in range(nsup):
                for s in relayed:
                    relay_copy(relay, s - relayed[0], k, s, w).wait_send()

    @pl.when(col != opposite)
    def _():
        for k in range(nsup):
            for s in relayed:
                cross_copy(k, s).wait_send()


def fused(ncol, ancestor_inverse, panels, block_lists, diag_inverse):
    nsup, depth, columns = panels.shape
    deep = diag_inverse.shape[1]
    tall = BS + ncol * deep
    crosses = CAP // CORES
    narrow, wide = panels.dtype, jnp.float32
    vmem = pl.BlockSpec(memory_space=pltpu.VMEM)
    dma = pltpu.SemaphoreType.DMA
    return pl.pallas_call(
        functools.partial(kernel, ncol),
        out_shape=(
            jax.ShapeDtypeStruct((nsup, BS, columns), narrow),
            jax.ShapeDtypeStruct(diag_inverse.shape, wide),
        ),
        in_specs=[pl.BlockSpec(memory_space=pltpu.SMEM), vmem, vmem, vmem],
        out_specs=(vmem, vmem),
        scratch_shapes=[
            tuple(pltpu.VMEM((CAP, BS, columns), narrow) for _ in range(nsup)),
            pltpu.VMEM((nsup, RELAYED, BS, columns), narrow),
            pltpu.VMEM((nsup, columns, depth), narrow),
            pltpu.VMEM((BPR, BS, columns), narrow),
            pltpu.VMEM((nsup, CORES, crosses, tall, columns), narrow),
            pltpu.VMEM((nsup, crosses, tall, columns), narrow),
            pltpu.VMEM((nsup, tall, columns), narrow),
            pltpu.VMEM((nsup, tall, columns), narrow),
            pltpu.VMEM((nsup, ncol, deep, columns), narrow),
            pltpu.VMEM((nsup, ncol, deep, columns), wide),
            pltpu.VMEM((nsup, ncol - 1, deep, columns), narrow),
            dma((nsup, CAP, 2)),
            dma((nsup, CAP)),
            dma((nsup, RELAYED, 2)),
            dma((nsup, RELAYED)),
            dma((nsup, RELAYED)),
            dma((nsup,)),
            dma((nsup,)),
            dma((nsup,)),
            dma((nsup,)),
            dma((nsup, ncol - 1)),
            dma((nsup, ncol - 1)),
            dma((nsup,)),
        ],
        compiler_params=pltpu.CompilerParams(
            collective_id=0, has_side_effects=True, vmem_limit_bytes=48 * 1024 * 1024
        ),
    )(
        block_lists,
        ancestor_inverse,
        panels.reshape(nsup, CAP, BS, columns),
        diag_inverse,
    )


def from_root(value, axis, source):
    kept = jnp.where(lax.axis_index(axis) == source, value, 0).astype(value.dtype)
    return lax.psum(kept, axis)


def complex_product(first, second):
    half = first.shape[1] // 2
    return jnp.concatenate(
        [first[:, :half] - second[:, half:], first[:, half:] + second[:, :half]], axis=1
    )


def on_device(ancestor_inverse, panels, block_lists, diag_inverse):
    here_col = lax.axis_index("col")
    here_row = lax.axis_index("row")
    nsup = panels.shape[0]
    width = panels.shape[2] // 2
    mine = lax.dynamic_slice_in_dim(block_lists, here_col * CAP, CAP, 1)
    theirs = lax.dynamic_slice_in_dim(block_lists, here_row * CAP, CAP, 1)
    row_mask = jnp.repeat((mine >= 0).astype(jnp.bfloat16), BS, axis=1)
    masked = panels * row_mask[:, :, None]
    blocks = ancestor_inverse.reshape(2, BPR, BS, BPR, BS)
    pieces = []
    for k in range(nsup):
        range_rows = from_root(masked[k], "col", here_row)
        row_offset = jnp.clip(mine[k] - here_col * BPR, 0, BPR - 1)
        col_offset = jnp.clip(theirs[k] - here_row * BPR, 0, BPR - 1)
        picked = jnp.take(blocks, row_offset, axis=1)
        picked = jnp.take(picked, col_offset, axis=3).reshape(2, CAP * BS, CAP * BS)
        product_first = jnp.dot(picked[0], range_rows, preferred_element_type=jnp.float32)
        product_second = jnp.dot(picked[1], range_rows, preferred_element_type=jnp.float32)
        pieces.append(
            lax.psum_scatter(
                (
                    complex_product(product_first, product_second)
                    * row_mask[k][:, None].astype(jnp.float32)
                ).astype(jnp.bfloat16),
                "row",
                scatter_dimension=0,
                tiled=True,
            ).astype(jnp.float32)
        )
    summed = jnp.stack(pieces)
    offdiag = (-summed).astype(jnp.bfloat16)
    share = summed.shape[1]
    own_rows = lax.dynamic_slice_in_dim(masked, here_row * share, share, 1)
    dims = (((0,), (0,)), ((), ()))
    updates = []
    for k in range(nsup):
        first = lax.dot_general(
            own_rows[k][:, :width], offdiag[k], dims, preferred_element_type=jnp.float32
        )
        second = lax.dot_general(
            own_rows[k][:, width:], offdiag[k], dims, preferred_element_type=jnp.float32
        )
        updates.append(complex_product(first, second))
    updates = jnp.stack(updates)
    own_update = lax.psum_scatter(updates, ("col", "row"), scatter_dimension=1, tiled=True)
    return (offdiag, diag_inverse - own_update)


def solution(mesh):
    ncol, nrow = mesh.shape["col"], mesh.shape["row"]

    def on_mesh(ancestor_inverse, panels, block_lists, diag_inverse):
        whole_slots = nrow == CAP and ncol == nrow
        if whole_slots and diag_inverse.shape[1] % 16 == 0:
            return fused(ncol, ancestor_inverse, panels, block_lists, diag_inverse)
        return on_device(ancestor_inverse, panels, block_lists, diag_inverse)

    return jax.shard_map(
        on_mesh,
        mesh=mesh,
        in_specs=(
            P("pole", "col", "row"),
            P("pole", "col", None),
            P("pole", None),
            P("pole", ("col", "row"), None),
        ),
        out_specs=(P("pole", ("col", "row"), None), P("pole", ("col", "row"), None)),
        check_vma=False,
    )
```

```python
import functools

import jax
import jax.numpy as jnp
from jax import lax
from jax.experimental import pallas as pl
from jax.experimental.pallas import tpu as pltpu
from jax.sharding import PartitionSpec as P

BS = 128
BPR = 4
CAP = 4
CORES = 2
RELAYED = 1
TURN = 1
MESH = pl.DeviceIdType.MESH


def kernel(
    ncol,
    lists,
    inverse_hbm,
    panels_hbm,
    diag_hbm,
    offdiag,
    diag_block,
    inverse,
    panels,
    diag_inverse,
    listed,
    relay,
    turned,
    term,
    parts,
    first_in,
    second_out,
    second_in,
    third_out,
    third_own,
    third_in,
    chain_send,
    chain_recv,
    relay_send,
    relay_recv,
    cross_send,
    first_send,
    first_recv,
    second_send,
    second_recv,
    third_send,
    third_recv,
    local_sem,
    load_sem,
):
    nsup = panels.shape[0]
    width = panels.shape[3] // 2
    loads = [
        pltpu.make_async_copy(source, target, load_sem.at[i])
        for i, (source, target) in enumerate(
            ((panels_hbm, panels), (inverse_hbm, inverse), (diag_hbm, diag_inverse))
        )
    ]
    for load in loads:
        load.start()
    deep = diag_inverse.shape[1]
    col = lax.axis_index("col")
    row = lax.axis_index("row")
    core = lax.rem(row, CORES)
    across = row // CORES
    sibling = across * CORES + (1 - core)
    opposite = (1 - across) * CORES + core
    main = range(CAP - RELAYED)
    relayed = range(CAP - RELAYED, CAP)
    ways = (1, -1)

    barrier = pltpu.get_barrier_semaphore()
    for other in (sibling, opposite):
        pl.semaphore_signal(barrier, inc=1, device_id={"row": other}, device_id_type=MESH)
    for step in range(1, ncol):
        pl.semaphore_signal(
            barrier, inc=1, device_id={"col": lax.rem(col + step, ncol)}, device_id_type=MESH
        )
    pl.semaphore_wait(barrier, ncol + 1)

    def along(source, target, send, recv, way):
        return pltpu.make_async_remote_copy(
            src_ref=source,
            dst_ref=target,
            send_sem=send,
            recv_sem=recv,
            device_id={"col": jnp.clip(col + way, 0, ncol - 1)},
            device_id_type=MESH,
        )

    def in_row(source, target, send, recv, other):
        return pltpu.make_async_remote_copy(
            src_ref=source,
            dst_ref=target,
            send_sem=send,
            recv_sem=recv,
            device_id={"row": other},
            device_id_type=MESH,
        )

    def room(way):
        return col < ncol - 1 if way > 0 else col > 0

    def beyond(origin, way):
        return col > origin if way > 0 else col < origin

    def far(origin, way):
        return origin < ncol // 2 if way > 0 else origin >= ncol // 2

    carries = (beyond(opposite, 1) & far(opposite, 1)) | (beyond(opposite, -1) & far(opposite, -1))

    def chain_copy(source, k, s, w):
        return along(
            source, listed[k].at[s], chain_send.at[k, s, w], chain_recv.at[k, s], ways[w]
        )

    def relay_copy(source, at, k, s, w):
        i = s - relayed[0]
        return along(
            source.at[k, at], relay.at[k, i], relay_send.at[k, i, w], relay_recv.at[k, i], ways[w]
        )

    def cross_copy(k, s):
        i = s - relayed[0]
        return in_row(relay.at[k, i], listed[k].at[s], cross_send.at[k, i], chain_recv.at[k, s], opposite)

    def own_copy(k):
        return pltpu.make_async_copy(panels_hbm.at[k], listed[k], local_sem.at[k])

    for k in range(nsup):
        for w, way in enumerate(ways):

            @pl.when((col == row) & room(way))
            def _():
                for s in main:
                    chain_copy(panels_hbm.at[k, s], k, s, w).start()

            @pl.when((col == row) & room(way) & jnp.logical_not(far(row, way)))
            def _():
                for s in relayed:
                    chain_copy(panels_hbm.at[k, s], k, s, w).start()

            @pl.when((col == opposite) & room(way) & far(opposite, way))
            def _():
                for s in relayed:
                    relay_copy(panels_hbm, s, k, s, w).start()

    @pl.when(col == row)
    def _():
        for k in range(nsup):
            own_copy(k).start()

    loads[0].wait()
    for k in range(nsup):
        rows = jnp.concatenate(
            [panels[k, x * CORES + c] for c in range(CORES) for x in range(CAP // CORES)], axis=0
        )
        turned[k] = rows.T

    @pl.when(col == row)
    def _():
        for k in range(nsup):
            own_copy(k).wait()

    loads[1].wait()
    loads[2].wait()

    def forward(k):
        for j in range(CAP):
            if j < len(main):
                s = main[j]

                @pl.when(col != row)
                def _():
                    chain_copy(listed[k].at[s], k, s, 0).wait_recv()

                for w, way in enumerate(ways):

                    @pl.when(beyond(row, way) & room(way))
                    def _():
                        chain_copy(listed[k].at[s], k, s, w).start()

            if j < len(relayed):
                s = relayed[j]

                @pl.when(carries)
                def _():
                    relay_copy(relay, s - relayed[0], k, s, 0).wait_recv()
                    cross_copy(k, s).start()

                for w, way in enumerate(ways):

                    @pl.when(beyond(opposite, way) & room(way) & far(opposite, way))
                    def _():
                        relay_copy(relay, s - relayed[0], k, s, w).start()

            if k > 0 and j == TURN:
                second_stage(k - 1)

        for s in relayed:

            @pl.when(col != row)
            def _():
                chain_copy(listed[k].at[s], k, s, 0).wait_recv()

            for w, way in enumerate(ways):

                @pl.when(beyond(row, way) & room(way) & jnp.logical_not(far(row, way)))
                def _():
                    chain_copy(listed[k].at[s], k, s, w).start()

    def first_copy(k):
        return in_row(
            parts.at[k, 1 - core], first_in.at[k], first_send.at[k], first_recv.at[k], sibling
        )

    def second_copy(k):
        return in_row(
            second_out.at[k], second_in.at[k], second_send.at[k], second_recv.at[k], opposite
        )

    def third_copy(k, step):
        target = lax.rem(col + step, ncol)
        return pltpu.make_async_remote_copy(
            src_ref=third_out.at[k, target],
            dst_ref=third_in.at[k, step - 1],
            send_sem=third_send.at[k, step - 1],
            recv_sem=third_recv.at[k, step - 1],
            device_id={"col": target},
            device_id_type=MESH,
        )

    def compute(k):
        natural = []
        for b in range(BPR):
            at = jnp.int32(0)
            found = jnp.int32(0)
            for s in range(CAP):
                hit = lists[k, row * CAP + s] == row * BPR + b
                at = jnp.where(hit, s, at)
                found = jnp.where(hit, 1, found)
            block = listed[k][at]
            natural.append(block * found.astype(jnp.float32).astype(block.dtype))
        natural = jnp.concatenate(natural, axis=0)
        both_planes = inverse[...].reshape(2 * BPR * BS, BPR * BS)
        product = jnp.dot(both_planes, natural, preferred_element_type=jnp.float32)
        first, second = product[: BPR * BS], product[BPR * BS :]
        term[:, :, :width] = (
            (first[:, :width] - second[:, width:]).astype(term.dtype).reshape(BPR, BS, width)
        )
        term[:, :, width:] = (
            (first[:, width:] + second[:, :width]).astype(term.dtype).reshape(BPR, BS, width)
        )
        slots = []
        for c in range(CORES):
            for x in range(CAP // CORES):
                block_id = lists[k, col * CAP + x * CORES + c]
                filled = (block_id >= 0).astype(jnp.float32).astype(term.dtype)
                piece = term[jnp.clip(block_id - col * BPR, 0, BPR - 1)] * filled
                parts[k, c, x, :BS] = piece
                slots.append(piece)
        slots = jnp.concatenate(slots, axis=0)
        update = jnp.dot(turned[k], slots, preferred_element_type=jnp.float32)
        first, second = update[:width], update[width:]
        update = jnp.concatenate(
            [first[:, :width] - second[:, width:], first[:, width:] + second[:, :width]], axis=1
        ).astype(parts.dtype)
        for z in range(ncol):
            for r in range(CAP):
                at = (z * CAP + r) * deep
                parts[k, r % CORES, r // CORES, BS + z * deep : BS + (z + 1) * deep] = update[at : at + deep]
        first_copy(k).start()

    def first_sum(k, x):
        return parts[k, core, x].astype(jnp.float32) + first_in[k, x].astype(jnp.float32)

    def second_stage(k):
        first_copy(k).wait_recv()
        second_out[k] = first_sum(k, 1 - across).astype(second_out.dtype)
        second_copy(k).start()

    def third_stage(k):
        second_copy(k).wait_recv()
        total = first_sum(k, across) + second_in[k].astype(jnp.float32)
        offdiag[k] = (-total[:BS]).astype(offdiag.dtype)
        third_own[k] = total[BS:].reshape(ncol, deep, 2 * width)
        third_out[k] = total[BS:].reshape(ncol, deep, 2 * width).astype(third_out.dtype)
        for step in range(1, ncol):
            third_copy(k, step).start()

    def last_stage(k):
        total = diag_inverse[k] + third_own[k, col]
        for step in range(1, ncol):
            third_copy(k, step).wait_recv()
            total += third_in[k, step - 1].astype(jnp.float32)
        diag_block[k] = total

    for k in range(nsup):
        forward(k)
        compute(k)
    second_stage(nsup - 1)
    for k in range(nsup):
        third_stage(k)
    for k in range(nsup):
        last_stage(k)

    for k in range(nsup):
        first_copy(k).wait_send()
        second_copy(k).wait_send()
        for step in range(1, ncol):
            third_copy(k, step).wait_send()
    for w, way in enumerate(ways):

        @pl.when((beyond(row, way) | (col == row)) & room(way))
        def _():
            for k in range(nsup):
                for s in main:
                    chain_copy(listed[k].at[s], k, s, w).wait_send()

        @pl.when((beyond(row, way) | (col == row)) & room(way) & jnp.logical_not(far(row, way)))
        def _():
            for k in range(nsup):
                for s in relayed:
                    chain_copy(listed[k].at[s], k, s, w).wait_send()

        @pl.when((beyond(opposite, way) | (col == opposite)) & room(way) & far(opposite, way))
        def _():
            for k in range(nsup):
                for s in relayed:
                    relay_copy(relay, s - relayed[0], k, s, w).wait_send()

    @pl.when(carries)
    def _():
        for k in range(nsup):
            for s in relayed:
                cross_copy(k, s).wait_send()


def fused(ncol, ancestor_inverse, panels, block_lists, diag_inverse):
    nsup, depth, columns = panels.shape
    deep = diag_inverse.shape[1]
    tall = BS + ncol * deep
    crosses = CAP // CORES
    narrow, wide = panels.dtype, jnp.float32
    vmem = pl.BlockSpec(memory_space=pltpu.VMEM)
    dma = pltpu.SemaphoreType.DMA
    return pl.pallas_call(
        functools.partial(kernel, ncol),
        out_shape=(
            jax.ShapeDtypeStruct((nsup, BS, columns), narrow),
            jax.ShapeDtypeStruct(diag_inverse.shape, wide),
        ),
        in_specs=[pl.BlockSpec(memory_space=pltpu.SMEM)] + [pl.BlockSpec(memory_space=pl.ANY)] * 3,
        out_specs=(vmem, vmem),
        scratch_shapes=[
            pltpu.VMEM(ancestor_inverse.shape, narrow),
            pltpu.VMEM((nsup, CAP, BS, columns), narrow),
            pltpu.VMEM(diag_inverse.shape, wide),
            tuple(pltpu.VMEM((CAP, BS, columns), narrow) for _ in range(nsup)),
            pltpu.VMEM((nsup, RELAYED, BS, columns), narrow),
            pltpu.VMEM((nsup, columns, depth), narrow),
            pltpu.VMEM((BPR, BS, columns), narrow),
            pltpu.VMEM((nsup, CORES, crosses, tall, columns), narrow),
            pltpu.VMEM((nsup, crosses, tall, columns), narrow),
            pltpu.VMEM((nsup, tall, columns), narrow),
            pltpu.VMEM((nsup, tall, columns), narrow),
            pltpu.VMEM((nsup, ncol, deep, columns), narrow),
            pltpu.VMEM((nsup, ncol, deep, columns), wide),
            pltpu.VMEM((nsup, ncol - 1, deep, columns), narrow),
            dma((nsup, CAP, 2)),
            dma((nsup, CAP)),
            dma((nsup, RELAYED, 2)),
            dma((nsup, RELAYED)),
            dma((nsup, RELAYED)),
            dma((nsup,)),
            dma((nsup,)),
            dma((nsup,)),
            dma((nsup,)),
            dma((nsup, ncol - 1)),
            dma((nsup, ncol - 1)),
            dma((nsup,)),
            dma((3,)),
        ],
        compiler_params=pltpu.CompilerParams(
            collective_id=0, has_side_effects=True, vmem_limit_bytes=48 * 1024 * 1024
        ),
    )(
        block_lists,
        ancestor_inverse,
        panels.reshape(nsup, CAP, BS, columns),
        diag_inverse,
    )


def from_root(value, axis, source):
    kept = jnp.where(lax.axis_index(axis) == source, value, 0).astype(value.dtype)
    return lax.psum(kept, axis)


def complex_product(first, second):
    half = first.shape[1] // 2
    return jnp.concatenate(
        [first[:, :half] - second[:, half:], first[:, half:] + second[:, :half]], axis=1
    )


def on_device(ancestor_inverse, panels, block_lists, diag_inverse):
    here_col = lax.axis_index("col")
    here_row = lax.axis_index("row")
    nsup = panels.shape[0]
    width = panels.shape[2] // 2
    mine = lax.dynamic_slice_in_dim(block_lists, here_col * CAP, CAP, 1)
    theirs = lax.dynamic_slice_in_dim(block_lists, here_row * CAP, CAP, 1)
    row_mask = jnp.repeat((mine >= 0).astype(jnp.bfloat16), BS, axis=1)
    masked = panels * row_mask[:, :, None]
    blocks = ancestor_inverse.reshape(2, BPR, BS, BPR, BS)
    pieces = []
    for k in range(nsup):
        range_rows = from_root(masked[k], "col", here_row)
        row_offset = jnp.clip(mine[k] - here_col * BPR, 0, BPR - 1)
        col_offset = jnp.clip(theirs[k] - here_row * BPR, 0, BPR - 1)
        picked = jnp.take(blocks, row_offset, axis=1)
        picked = jnp.take(picked, col_offset, axis=3).reshape(2, CAP * BS, CAP * BS)
        product_first = jnp.dot(picked[0], range_rows, preferred_element_type=jnp.float32)
        product_second = jnp.dot(picked[1], range_rows, preferred_element_type=jnp.float32)
        pieces.append(
            lax.psum_scatter(
                (
                    complex_product(product_first, product_second)
                    * row_mask[k][:, None].astype(jnp.float32)
                ).astype(jnp.bfloat16),
                "row",
                scatter_dimension=0,
                tiled=True,
            ).astype(jnp.float32)
        )
    summed = jnp.stack(pieces)
    offdiag = (-summed).astype(jnp.bfloat16)
    share = summed.shape[1]
    own_rows = lax.dynamic_slice_in_dim(masked, here_row * share, share, 1)
    dims = (((0,), (0,)), ((), ()))
    updates = []
    for k in range(nsup):
        first = lax.dot_general(
            own_rows[k][:, :width], offdiag[k], dims, preferred_element_type=jnp.float32
        )
        second = lax.dot_general(
            own_rows[k][:, width:], offdiag[k], dims, preferred_element_type=jnp.float32
        )
        updates.append(complex_product(first, second))
    updates = jnp.stack(updates)
    own_update = lax.psum_scatter(updates, ("col", "row"), scatter_dimension=1, tiled=True)
    return (offdiag, diag_inverse - own_update)


def solution(mesh):
    ncol, nrow = mesh.shape["col"], mesh.shape["row"]

    def on_mesh(ancestor_inverse, panels, block_lists, diag_inverse):
        whole_slots = nrow == CAP and ncol == nrow
        if whole_slots and diag_inverse.shape[1] % 16 == 0:
            return fused(ncol, ancestor_inverse, panels, block_lists, diag_inverse)
        return on_device(ancestor_inverse, panels, block_lists, diag_inverse)

    return jax.shard_map(
        on_mesh,
        mesh=mesh,
        in_specs=(
            P("pole", "col", "row"),
            P("pole", "col", None),
            P("pole", None),
            P("pole", ("col", "row"), None),
        ),
        out_specs=(P("pole", ("col", "row"), None), P("pole", ("col", "row"), None)),
        check_vma=False,
    )
```
